32 devices in a mesh: section: 2 (over core), peer: 16 (over z, y, x).
Axes of the slice: x: 2, y: 2, z: 4, core: 2. Of those that a mesh axis runs over, the one named last changes fastest.
Arguments:
- arrivals: bfloat16 [2, 16, 64, 5120], P('section', 'peer'), may hold values from -6 to 6
- kept: bfloat16 [2, 16, 64, 5120], P('section', 'peer'), may hold values from -8 to 8
- returned: bfloat16 [2, 16, 64, 5120], P('section', 'peer'), may hold values from -8 to 8
- onward: int32 [2, 16], P('section'), may hold values from 0 to 15, each once within a row
- backward_route: int32 [2, 16], P('section'), may hold values from 0 to 15, each once within a row
- replicas: bfloat16 [2, 16, 5120, 128], P('section', 'peer'), may hold values from -6 to 6
- master: float32 [2, 5120, 128], P('section', 'peer'), may hold values from -0.6 to 0.6
- moment: float32 [2, 5120, 128], P('section', 'peer'), may hold values from -4 to 4
- second: float32 [2, 5120, 128], P('section', 'peer'), may hold values from 0.1 to 10
Outputs:
- handed_on: bfloat16 [2, 16, 64, 5120], P('section', 'peer')
- passed_back: bfloat16 [2, 16, 64, 5120], P('section', 'peer')
- new_master: float32 [2, 5120, 128], P('section', 'peer')
- new_moment: float32 [2, 5120, 128], P('section', 'peer')
- new_second: float32 [2, 5120, 128], P('section', 'peer')
The draws below stay inside these ranges and needn't reach their ends.
Inputs may be any that keep to these rules, and one draw needn't show every extreme that they name: `onward`: each row lists every peer index once. `backward_route`: each row lists every peer index once.
All inputs are finite; a program needn't handle non-finite values.
Results may differ from the reference program's by a relative error of at most 0.004.
Values may be sent and summed in bfloat16 or wider, within the bound.
A program may use at most 64 MiB of HBM per device.

```python
import math
import jax
import jax.numpy as jnp
from jax import lax

D = 5120
RANK = 64
TOK = 64
SECTIONS = 2
PEERS = 16


def shared_factors(key):
    weights = jax.random.normal(jax.random.fold_in(key, 71), (SECTIONS, PEERS, D, 2 * RANK), jnp.float32)
    weights = jnp.clip(weights, -6.0, 6.0)
    coefficients = jax.random.normal(jax.random.fold_in(key, 72), (SECTIONS, PEERS, TOK, RANK), jnp.float32)
    return (weights, coefficients)


def drawn_part(coefficients, columns, factor):
    spanned = jnp.einsum('sptr,spdr->sptd', coefficients, columns, precision=lax.Precision.HIGHEST)
    return spanned * (factor / math.sqrt(RANK))


def draw_replicas(key, part):
    weights, coefficients = shared_factors(key)
    return weights.astype(jnp.bfloat16)


def draw_kept(key, part):
    weights, coefficients = shared_factors(key)
    key = jax.random.fold_in(key, 2)
    shape = (SECTIONS, PEERS, TOK, D)
    noise = jnp.clip(jax.random.normal(key, shape, jnp.float32), -6.0, 6.0)
    values = noise + drawn_part(coefficients, weights[..., :RANK], 0.3)
    return jnp.clip(values, -8.0, 8.0).astype(jnp.bfloat16)


def draw_returned(key, part):
    weights, coefficients = shared_factors(key)
    key = jax.random.fold_in(key, 3)
    shape = (SECTIONS, PEERS, TOK, D)
    noise = jnp.clip(jax.random.normal(key, shape, jnp.float32), -6.0, 6.0)
    values = noise + drawn_part(coefficients, weights[..., RANK:], 0.1)
    return jnp.clip(values, -8.0, 8.0).astype(jnp.bfloat16)


def block_levels(stream_key, dims, split, smallest, high):
    level = 1.0
    for axis_at, blocks in split:
        draws = jax.random.uniform(jax.random.fold_in(jax.random.fold_in(stream_key, 6), axis_at), (blocks,), jnp.float32, smallest / len(split), high / len(split))
        level = level * jnp.repeat(jnp.exp(draws), dims[axis_at] // blocks).reshape((-1,) + (1,) * (len(dims) - 1 - axis_at))
    return level


def scatter_about(stream_key, dims, spread, most, cuts=(), held_as=jnp.bfloat16):
    gain = block_levels(stream_key, dims, cuts, -0.22, 0.18) if cuts else 1.0
    drawn = jax.random.normal(stream_key, dims, jnp.float32) * spread * gain
    return jnp.minimum(jnp.maximum(drawn, -most), most).astype(held_as)


def setup_inputs(seed: int = 0) -> dict:
    keys = jax.random.split(jax.random.key(seed), 10)
    arrivals = scatter_about(keys[0], (SECTIONS, PEERS, TOK, D), 1.0, 6.0, ((0, 2), (1, 16)))
    kept = draw_kept(jax.random.fold_in(keys[9], 71), 0)
    returned = draw_returned(jax.random.fold_in(keys[9], 71), 0)
    onward = jax.vmap(lambda own: jax.random.permutation(own, PEERS))(jax.random.split(keys[3], SECTIONS)).reshape((SECTIONS, PEERS)).astype(jnp.int32)
    backward_route = jax.vmap(lambda own: jax.random.permutation(own, PEERS))(jax.random.split(keys[4], SECTIONS)).reshape((SECTIONS, PEERS)).astype(jnp.int32)
    replicas = draw_replicas(jax.random.fold_in(keys[9], 71), 0)
    master = scatter_about(keys[6], (SECTIONS, D, 2 * RANK), 0.1, 0.6, ((0, 2), (1, 16)), jnp.float32)
    moment = scatter_about(keys[7], (SECTIONS, D, 2 * RANK), 0.5, 4.0, ((0, 2), (1, 16)), jnp.float32)
    second = jnp.clip(jnp.exp(math.log(10.0) - 4.6051702 * jax.random.uniform(keys[8], (SECTIONS, D, 2 * RANK), jnp.float32) ** block_levels(keys[8], (SECTIONS, D, 2 * RANK), ((0, 2), (1, 16)), -0.2, 0.2)), 0.1, 10.0)
    return dict(arrivals=arrivals, kept=kept, returned=returned, onward=onward, backward_route=backward_route, replicas=replicas, master=master, moment=moment, second=second)


norm_eps = 1e-05
beta_first = 0.9
beta_second = 0.95
adam_eps = 1e-08
learn_rate = 0.05
weight_decay = 0.1
first_correction = 1.0 - 0.9 ** 10
second_correction = 1.0 - 0.95 ** 10

def norm_rate(values):
    return lax.rsqrt(lax.optimization_barrier(jnp.mean(values * values, axis=-1, keepdims=True)) + norm_eps)

def widen(narrow):
    return lax.optimization_barrier(narrow).astype(jnp.float32)

def forward_batch(tokens, weights):
    inner_rank = weights.shape[2] // 2
    features = tokens.shape[2]
    values = tokens.astype(jnp.float32)
    normed = widen((values * norm_rate(values)).astype(jnp.bfloat16))
    up_weight = weights[:, :, :inner_rank].astype(jnp.float32)
    down_weight = weights[:, :, inner_rank:].astype(jnp.float32)
    hidden = jnp.einsum('ptd,pdr->ptr', normed, up_weight, precision=lax.Precision.HIGHEST) * features ** (-0.5)
    active = widen(jax.nn.silu(hidden).astype(jnp.bfloat16))
    branch = jnp.einsum('ptr,pdr->ptd', active, down_weight, precision=lax.Precision.HIGHEST)
    return (values + branch * inner_rank ** (-0.5)).astype(jnp.bfloat16)

def backward_batch(tokens, weights, upstream):
    inner_rank = weights.shape[2] // 2
    features = tokens.shape[2]
    values = tokens.astype(jnp.float32)
    scaling = norm_rate(values)
    normed = widen((values * scaling).astype(jnp.bfloat16))
    up_weight = weights[:, :, :inner_rank].astype(jnp.float32)
    down_weight = weights[:, :, inner_rank:].astype(jnp.float32)
    upstream_wide = upstream.astype(jnp.float32)
    hidden = jnp.einsum('ptd,pdr->ptr', normed, up_weight, precision=lax.Precision.HIGHEST) * features ** (-0.5)
    active = widen(jax.nn.silu(hidden).astype(jnp.bfloat16))
    grad_active = jnp.einsum('ptd,pdr->ptr', upstream_wide, down_weight, precision=lax.Precision.HIGHEST) * inner_rank ** (-0.5)
    logistic = jax.nn.sigmoid(hidden)
    grad_hidden = widen((grad_active * logistic * (1.0 + hidden * (1.0 - logistic))).astype(jnp.bfloat16))
    grad_down = jnp.einsum('ptd,ptr->dr', upstream_wide, active, precision=lax.Precision.HIGHEST) * inner_rank ** (-0.5)
    grad_up = jnp.einsum('ptd,ptr->dr', normed, grad_hidden, precision=lax.Precision.HIGHEST) * features ** (-0.5)
    grad_normed = jnp.einsum('ptr,pdr->ptd', grad_hidden, up_weight, precision=lax.Precision.HIGHEST) * features ** (-0.5)
    mixed = lax.optimization_barrier(jnp.mean(grad_normed * values, axis=-1, keepdims=True))
    grad_tokens = upstream_wide + scaling * grad_normed - values * scaling ** 3 * mixed
    return (grad_tokens.astype(jnp.bfloat16), jnp.concatenate([grad_up, grad_down], axis=1))

def reference(arrivals, kept, returned, onward, backward_route, replicas, master, moment, second):
    sections = arrivals.shape[0]
    handed = jnp.zeros_like(arrivals)
    passed = jnp.zeros_like(arrivals)
    gradients = []
    for section_index in range(sections):
        produced = forward_batch(arrivals[section_index], replicas[section_index])
        handed = handed.at[(section_index + 1) % sections, onward[section_index]].set(produced)
        grad_tokens, gradient = backward_batch(kept[section_index], replicas[section_index], returned[section_index])
        passed = passed.at[(section_index - 1) % sections, backward_route[section_index]].set(grad_tokens)
        gradients.append(gradient)
    gradient = jnp.stack(gradients)
    new_moment = beta_first * moment + (1.0 - beta_first) * gradient
    new_second = beta_second * second + (1.0 - beta_second) * gradient * gradient
    update = new_moment / first_correction / (jnp.sqrt(new_second / second_correction) + adam_eps)
    new_master = master - learn_rate * (update + weight_decay * master)
    return (handed, passed, new_master, new_moment, new_second)
```

```python
import functools
import math

import jax
import jax.numpy as jnp
from jax import lax
from jax.experimental import pallas as pl
from jax.experimental.pallas import tpu as pltpu
from jax.sharding import PartitionSpec as P

norm_eps = 1e-05
beta_first = 0.9
beta_second = 0.95
adam_eps = 1e-08
learn_rate = 0.05
weight_decay = 0.1
first_correction = 1.0 - 0.9**10
second_correction = 1.0 - 0.95**10

ROWS = 16
MESH = pl.DeviceIdType.MESH
F32, BF16 = jnp.float32, jnp.bfloat16


def inverse_order(targets):
    positions = jnp.arange(targets.shape[0], dtype=jnp.int32)
    matches = (targets[:, None] == positions[None, :]).astype(jnp.int32)
    return jnp.sum(matches * positions[:, None], axis=0)


def column_chunks(width, parts):
    step = width // parts
    return [(i * step, step) for i in range(parts)]


def kernel(
    sections, peers, inner, width,
    source_on, source_back, arrivals, kept, returned, weights, master, moment, second,
    handed, passed, new_master, new_moment, new_second,
    made, landed_on, landed_back, outgoing, grad_normed, stacked, grad_wide, grad_sent, grad_landed,
    part_wide, part_sent, part_landed, sems,
):
    token_count, features = arrivals.shape
    rank = weights.shape[1] // 2
    outer = peers // inner
    col_groups = peers // (token_count // ROWS)
    shard = master.shape[0]
    sec, me = lax.axis_index("section"), lax.axis_index("peer")
    plane, spot = me // inner, lax.rem(me, inner)
    onto = lax.rem(sec + 1, sections)
    back = lax.rem(sec + sections - 1, sections)

    landings = (landed_on, landed_back)
    barrier = pltpu.get_barrier_semaphore()

    def greet(section, first):
        def one(k, carry):
            target = lax.rem(me + k, peers)
            pl.semaphore_signal(barrier, inc=1, device_id=(section, target), device_id_type=MESH)
            return carry
        lax.fori_loop(first, peers, one, 0)

    greet(sec, 1)
    greet(onto, 0)
    greeted = 2 * peers - 1
    if sections > 2:
        greet(back, 0)
        greeted += peers

    def piece(j):
        row = pl.multiple_of((j // col_groups) * ROWS, ROWS)
        col = pl.multiple_of(lax.rem(j, col_groups) * width, 128)
        return pl.ds(row, ROWS), pl.ds(col, width)

    def spread(t):
        def one(k, carry):
            j = lax.rem(me + k, peers)
            rows, cols = piece(j)
            pltpu.make_async_remote_copy(
                made.at[t, rows, cols], landings[t].at[me], sems.at[t], sems.at[2 + t],
                device_id=(sec, j), device_id_type=MESH,
            ).start()
            return carry
        lax.fori_loop(1, peers, one, 0)
        rows, cols = piece(me)
        pltpu.make_async_copy(made.at[t, rows, cols], landings[t].at[me], sems.at[2 + t]).start()

    def collect(t, order, section, result):
        pltpu.make_async_copy(landings[t], landings[t], sems.at[2 + t]).wait()
        rows, cols = piece(me)

        def one(k, carry):
            d = lax.rem(me + k, peers)
            outgoing[t, d] = landings[t][order[d]]
            pltpu.make_async_remote_copy(
                outgoing.at[t, d], result.at[rows, cols], sems.at[4 + t], sems.at[6 + t],
                device_id=(section, d), device_id_type=MESH,
            ).start()
            return carry
        lax.fori_loop(0, peers, one, 0)

    chunks = column_chunks(features, 4)
    if made.shape[2] > features:
        made[:, :, features:] = jnp.zeros((2, token_count, made.shape[2] - features), BF16)

    def rate(ref):
        total = jnp.zeros((token_count, 128), F32)
        for start, size in chunks:
            x = ref[:, start:start + size].astype(F32)
            x = x * x
            for c in range(0, size, 128):
                total += x[:, c:c + 128]
        return lax.rsqrt(jnp.sum(total, axis=1, keepdims=True) * (1.0 / features) + norm_eps)

    right = lax.broadcasted_iota(jnp.int32, (token_count, 2 * rank), 1) >= rank
    nt = (((1,), (1,)), ((), ()))

    r = rate(arrivals)
    hidden = jnp.zeros((token_count, 2 * rank), F32)
    for start, size in chunks:
        normed = (arrivals[:, start:start + size].astype(F32) * r).astype(BF16)
        hidden += jnp.dot(normed, weights[start:start + size, :], preferred_element_type=F32)
    hidden = hidden * features ** (-0.5)
    active = hidden / (1.0 + jnp.exp(-hidden))
    active = jnp.where(right, pltpu.roll(active, rank, 1), 0.0).astype(BF16)
    for start, size in chunks:
        branch = lax.dot_general(active, weights[start:start + size, :], nt, preferred_element_type=F32)
        y = arrivals[:, start:start + size].astype(F32) + branch * rank ** (-0.5)
        made[0, :, start:start + size] = y.astype(BF16)
    pl.semaphore_wait(barrier, greeted)
    spread(0)

    r = rate(kept)
    both = jnp.zeros((2 * token_count, 2 * rank), F32)
    for start, size in chunks:
        normed = (kept[:, start:start + size].astype(F32) * r).astype(BF16)
        stacked[:token_count, start:start + size] = normed
        stacked[token_count:, start:start + size] = returned[:, start:start + size]
        both += jnp.dot(stacked[:, start:start + size], weights[start:start + size, :], preferred_element_type=F32)
    hidden = both[:token_count] * features ** (-0.5)
    grad_active = pltpu.roll(both[token_count:], rank, 1) * rank ** (-0.5)
    logistic = 1.0 / (1.0 + jnp.exp(-hidden))
    active = jnp.where(right, pltpu.roll(hidden * logistic, rank, 1), 0.0).astype(BF16)
    grad_hidden = grad_active * logistic * (1.0 + hidden * (1.0 - logistic))
    grad_hidden = jnp.where(right, 0.0, grad_hidden).astype(BF16)
    mixed = jnp.zeros((token_count, 128), F32)
    for start, size in chunks:
        g = lax.dot_general(grad_hidden, weights[start:start + size, :], nt, preferred_element_type=F32)
        g = g * features ** (-0.5)
        grad_normed[:, start:start + size] = g
        g = g * kept[:, start:start + size].astype(F32)
        for c in range(0, size, 128):
            mixed += g[:, c:c + 128]
    mixed = jnp.sum(mixed, axis=1, keepdims=True) * (1.0 / features)
    pull = r * r * r * mixed
    for start, size in chunks:
        dx = (
            returned[:, start:start + size].astype(F32)
            + r * grad_normed[:, start:start + size]
            - kept[:, start:start + size].astype(F32) * pull
        )
        made[1, :, start:start + size] = dx.astype(BF16)
    spread(1)

    factors = jnp.concatenate([grad_hidden, active], axis=0)
    scale = jnp.where(
        lax.broadcasted_iota(jnp.int32, (1, 2 * rank), 1) >= rank, rank ** (-0.5), features ** (-0.5)
    )
    step = math.lcm(shard, 128)
    for start in range(0, features, step):
        g = lax.dot_general(
            stacked[:, start:start + step], factors, (((0,), (0,)), ((), ())), preferred_element_type=F32
        ) * scale
        for i in range(step // shard):
            j = start // shard + i
            z, q = divmod(j, inner)
            rows = g[i * shard:(i + 1) * shard]
            grad_wide[q, z * shard:(z + 1) * shard] = rows
            grad_sent[q, z * shard:(z + 1) * shard] = rows.astype(BF16)

    def send_plane(k, carry):
        q = lax.rem(spot + k, inner)
        pltpu.make_async_remote_copy(
            grad_sent.at[q], grad_landed.at[spot], sems.at[8], sems.at[9],
            device_id=(sec, plane * inner + q), device_id_type=MESH,
        ).start()
        return carry
    lax.fori_loop(1, inner, send_plane, 0)

    collect(0, source_on, onto, handed)

    less = pl.ds(0, inner - 1)
    pltpu.make_async_copy(grad_sent.at[less], grad_landed.at[less], sems.at[9]).wait()
    for z in range(outer):
        rows = pl.ds(z * shard, shard)
        total = grad_wide[spot, rows]
        for k in range(1, inner):
            total += grad_landed[lax.rem(spot + k, inner), rows].astype(F32)
        part_wide[z] = total
        part_sent[z] = total.astype(BF16)

    def send_line(k, carry):
        z = lax.rem(plane + k, outer)
        pltpu.make_async_remote_copy(
            part_sent.at[z], part_landed.at[plane], sems.at[10], sems.at[11],
            device_id=(sec, z * inner + spot), device_id_type=MESH,
        ).start()
        return carry
    lax.fori_loop(1, outer, send_line, 0)

    collect(1, source_back, back, passed)

    few = pl.ds(0, outer - 1)
    pltpu.make_async_copy(part_sent.at[few], part_landed.at[few], sems.at[11]).wait()
    grad = part_wide[plane]
    for k in range(1, outer):
        grad += part_landed[lax.rem(plane + k, outer)].astype(F32)
    first = beta_first * moment[...] + (1.0 - beta_first) * grad
    other = beta_second * second[...] + (1.0 - beta_second) * grad * grad
    update = first / first_correction / (jnp.sqrt(other / second_correction) + adam_eps)
    new_moment[...] = first
    new_second[...] = other
    new_master[...] = master[...] - learn_rate * (update + weight_decay * master[...])

    most = pl.ds(0, peers - 1)
    for t, result in ((0, handed), (1, passed)):
        pltpu.make_async_copy(landings[t].at[most], landings[t].at[most], sems.at[t]).wait()
        pltpu.make_async_copy(outgoing.at[t], outgoing.at[t], sems.at[4 + t]).wait()
        pltpu.make_async_copy(result, result, sems.at[6 + t]).wait()
    pltpu.make_async_copy(grad_sent.at[less], grad_sent.at[less], sems.at[8]).wait()
    pltpu.make_async_copy(part_sent.at[few], part_sent.at[few], sems.at[10]).wait()


def plane_size(peers):
    size = 1
    while size * size < peers:
        size *= 2
    return size


def shards(sections, arrivals, kept, returned, onward, backward_route, replicas, master, moment, second):
    peers = lax.axis_size("peer")
    token_count, features = arrivals.shape[2:]
    lanes = replicas.shape[3]
    shard = master.shape[1]
    inner = plane_size(peers)
    outer = peers // inner
    col_groups = peers // (token_count // ROWS)
    width = -(-features // (col_groups * 128)) * 128
    padded = width * col_groups
    vmem = pl.BlockSpec(memory_space=pltpu.VMEM)
    smem = pl.BlockSpec(memory_space=pltpu.SMEM)
    rows = jax.ShapeDtypeStruct((shard, lanes), F32)
    block = jax.ShapeDtypeStruct((token_count, padded), BF16)
    handed, passed, new_master, new_moment, new_second = pl.pallas_call(
        functools.partial(kernel, sections, peers, inner, width),
        out_shape=(block, block, rows, rows, rows),
        in_specs=[smem] * 2 + [vmem] * 7,
        out_specs=(vmem,) * 5,
        scratch_shapes=[
            pltpu.VMEM((2, token_count, padded), BF16),
            pltpu.VMEM((peers, ROWS, width), BF16),
            pltpu.VMEM((peers, ROWS, width), BF16),
            pltpu.VMEM((2, peers, ROWS, width), BF16),
            pltpu.VMEM((token_count, features), F32),
            pltpu.VMEM((2 * token_count, features), BF16),
            pltpu.VMEM((inner, outer * shard, lanes), F32),
            pltpu.VMEM((inner, outer * shard, lanes), BF16),
            pltpu.VMEM((inner, outer * shard, lanes), BF16),
            pltpu.VMEM((outer, shard, lanes), F32),
            pltpu.VMEM((outer, shard, lanes), BF16),
            pltpu.VMEM((outer, shard, lanes), BF16),
            pltpu.SemaphoreType.DMA((12,)),
        ],
        compiler_params=pltpu.CompilerParams(
            collective_id=0, has_side_effects=True, vmem_limit_bytes=48 * 1024 * 1024
        ),
        name="routed_step",
    )(
        inverse_order(onward[0]), inverse_order(backward_route[0]),
        arrivals[0, 0], kept[0, 0], returned[0, 0], replicas[0, 0], master[0], moment[0], second[0],
    )
    return (
        handed[None, None, :, :features], passed[None, None, :, :features],
        new_master[None], new_moment[None], new_second[None],
    )


def solution(mesh):
    whole = P("section", "peer", None, None)
    rows = P("section", "peer", None)
    table = P("section", None)
    return jax.shard_map(
        functools.partial(shards, mesh.shape["section"]),
        mesh=mesh,
        in_specs=(whole, whole, whole, table, table, whole, rows, rows, rows),
        out_specs=(whole, whole, rows, rows, rows),
        check_vma=False,
    )
```

```python
import functools
import math

import jax
import jax.numpy as jnp
from jax import lax
from jax.experimental import pallas as pl
from jax.experimental.pallas import tpu as pltpu
from jax.sharding import PartitionSpec as P

norm_eps = 1e-05
beta_first = 0.9
beta_second = 0.95
adam_eps = 1e-08
learn_rate = 0.05
weight_decay = 0.1
first_correction = 1.0 - 0.9**10
second_correction = 1.0 - 0.95**10

ROWS = 16
MESH = pl.DeviceIdType.MESH
F32, BF16 = jnp.float32, jnp.bfloat16


def column_chunks(width, parts):
    step = width // parts
    return [(i * step, step) for i in range(parts)]


def kernel(
    sections, peers, inner, width,
    table_on, table_back, *refs,
):
    operands, refs = refs[:7], refs[7:]
    results, refs = refs[:5], refs[5:]
    staged, refs = refs[:7], refs[7:]
    step(sections, peers, inner, width, table_on, table_back, operands, *staged, *results, *refs)


def step(
    sections, peers, inner, width, table_on, table_back, operands,
    arrivals, kept, returned, weights, master, moment, second,
    handed, passed, new_master, new_moment, new_second,
    made, landed_on, landed_back, outgoing, grad_normed, stacked, grad_wide, grad_sent, grad_landed,
    part_wide, part_sent, part_landed, far_wide, far_sent, far_landed,
    first_out, second_out, master_out, source_on, source_back, load_sems, sems,
):
    token_count, features = arrivals.shape
    rank = weights.shape[1] // 2
    outer = peers // inner
    col_groups = peers // (token_count // ROWS)
    shard = master.shape[0]
    sec, me = lax.axis_index("section"), lax.axis_index("peer")
    plane, spot = me // inner, lax.rem(me, inner)
    onto = lax.rem(sec + 1, sections)
    back = lax.rem(sec + sections - 1, sections)

    loads = [
        pltpu.make_async_copy(operand, here, load_sems.at[i])
        for i, (operand, here) in enumerate(
            zip(operands, (arrivals, kept, returned, weights, master, moment, second))
        )
    ]
    for i in (0, 3, 1, 2, 4, 5, 6):
        loads[i].start()
    landings = (landed_on, landed_back)
    barrier = pltpu.get_barrier_semaphore()

    def greet(section, first):
        def one(k, carry):
            target = lax.rem(me + k, peers)
            pl.semaphore_signal(barrier, inc=1, device_id=(section, target), device_id_type=MESH)
            return carry
        lax.fori_loop(first, peers, one, 0)

    greet(sec, 1)
    greet(onto, 0)
    greeted = 2 * peers - 1
    if sections > 2:
        greet(back, 0)
        greeted += peers

    def piece(j):
        row = pl.multiple_of((j // col_groups) * ROWS, ROWS)
        col = pl.multiple_of(lax.rem(j, col_groups) * width, 128)
        return pl.ds(row, ROWS), pl.ds(col, width)

    def spread(t):
        def one(k, carry):
            j = lax.rem(me + k, peers)
            rows, cols = piece(j)
            pltpu.make_async_remote_copy(
                made.at[t, rows, cols], landings[t].at[me], sems.at[t], sems.at[2 + t],
                device_id=(sec, j), device_id_type=MESH,
            ).start()
            return carry
        lax.fori_loop(1, peers, one, 0)
        rows, cols = piece(me)
        pltpu.make_async_copy(made.at[t, rows, cols], landings[t].at[me], sems.at[2 + t]).start()

    def collect(t, order, section, result):
        pltpu.make_async_copy(landings[t], landings[t], sems.at[2 + t]).wait()
        rows, cols = piece(me)

        def one(k, carry):
            d = lax.rem(me + k, peers)
            outgoing[t, d] = landings[t][order[d]]
            pltpu.make_async_remote_copy(
                outgoing.at[t, d], result.at[rows, cols], sems.at[4 + t], sems.at[6 + t],
                device_id=(section, d), device_id_type=MESH,
            ).start()
            return carry
        lax.fori_loop(0, peers, one, 0)

    def invert(table, order):
        def one(d, carry):
            found = jnp.int32(0)
            for p in range(1, peers):
                found = jnp.where(table[p] == d, p, found)
            order[d] = found
            return carry
        lax.fori_loop(0, peers, one, 0)

    chunks = column_chunks(features, 4)
    if made.shape[2] > features:
        made[:, :, features:] = jnp.zeros((2, token_count, made.shape[2] - features), BF16)

    def rate(ref):
        total = jnp.zeros((token_count, 128), F32)
        for start, size in chunks:
            x = ref[:, start:start + size].astype(F32)
            x = x * x
            for c in range(0, size, 128):
                total += x[:, c:c + 128]
        return lax.rsqrt(jnp.sum(total, axis=1, keepdims=True) * (1.0 / features) + norm_eps)

    right = lax.broadcasted_iota(jnp.int32, (token_count, 2 * rank), 1) >= rank
    nt = (((1,), (1,)), ((), ()))

    loads[0].wait()
    r = rate(arrivals)
    loads[3].wait()
    hidden = jnp.zeros((token_count, 2 * rank), F32)
    for start, size in chunks:
        normed = (arrivals[:, start:start + size].astype(F32) * r).astype(BF16)
        hidden += jnp.dot(normed, weights[start:start + size, :], preferred_element_type=F32)
    hidden = hidden * features ** (-0.5)
    active = hidden / (1.0 + jnp.exp(-hidden))
    active = jnp.where(right, pltpu.roll(active, rank, 1), 0.0).astype(BF16)
    for start, size in chunks:
        branch = lax.dot_general(active, weights[start:start + size, :], nt, preferred_element_type=F32)
        y = arrivals[:, start:start + size].astype(F32) + branch * rank ** (-0.5)
        made[0, :, start:start + size] = y.astype(BF16)
    pl.semaphore_wait(barrier, greeted)
    spread(0)

    loads[1].wait()
    loads[2].wait()
    r = rate(kept)
    both = jnp.zeros((2 * token_count, 2 * rank), F32)
    for start, size in chunks:
        normed = (kept[:, start:start + size].astype(F32) * r).astype(BF16)
        stacked[:token_count, start:start + size] = normed
        stacked[token_count:, start:start + size] = returned[:, start:start + size]
        both += jnp.dot(stacked[:, start:start + size], weights[start:start + size, :], preferred_element_type=F32)
    hidden = both[:token_count] * features ** (-0.5)
    grad_active = pltpu.roll(both[token_count:], rank, 1) * rank ** (-0.5)
    logistic = 1.0 / (1.0 + jnp.exp(-hidden))
    active = jnp.where(right, pltpu.roll(hidden * logistic, rank, 1), 0.0).astype(BF16)
    grad_hidden = grad_active * logistic * (1.0 + hidden * (1.0 - logistic))
    grad_hidden = jnp.where(right, 0.0, grad_hidden).astype(BF16)
    mixed = jnp.zeros((token_count, 128), F32)
    for start, size in chunks:
        g = lax.dot_general(grad_hidden, weights[start:start + size, :], nt, preferred_element_type=F32)
        g = g * features ** (-0.5)
        grad_normed[:, start:start + size] = g
        g = g * kept[:, start:start + size].astype(F32)
        for c in range(0, size, 128):
            mixed += g[:, c:c + 128]
    mixed = jnp.sum(mixed, axis=1, keepdims=True) * (1.0 / features)
    pull = r * r * r * mixed
    for start, size in chunks:
        dx = (
            returned[:, start:start + size].astype(F32)
            + r * grad_normed[:, start:start + size]
            - kept[:, start:start + size].astype(F32) * pull
        )
        made[1, :, start:start + size] = dx.astype(BF16)
    spread(1)

    factors = jnp.concatenate([grad_hidden, active], axis=0)
    scale = jnp.where(
        lax.broadcasted_iota(jnp.int32, (1, 2 * rank), 1) >= rank, rank ** (-0.5), features ** (-0.5)
    )
    step = math.lcm(shard, 128)
    for start in range(0, features, step):
        g = lax.dot_general(
            stacked[:, start:start + step], factors, (((0,), (0,)), ((), ())), preferred_element_type=F32
        ) * scale
        for i in range(step // shard):
            j = start // shard + i
            z, q = divmod(j, inner)
            rows = g[i * shard:(i + 1) * shard]
            grad_wide[q, z * shard:(z + 1) * shard] = rows
            grad_sent[q, z * shard:(z + 1) * shard] = rows.astype(BF16)

    def send_plane(k, carry):
        q = lax.rem(spot + k, inner)
        pltpu.make_async_remote_copy(
            grad_sent.at[q], grad_landed.at[spot], sems.at[8], sems.at[9],
            device_id=(sec, plane * inner + q), device_id_type=MESH,
        ).start()
        return carry
    lax.fori_loop(1, inner, send_plane, 0)

    invert(table_on, source_on)
    invert(table_back, source_back)
    collect(0, source_on, onto, handed)

    parity, pair = lax.rem(plane, 2), plane // 2
    less = pl.ds(0, inner - 1)
    pltpu.make_async_copy(grad_sent.at[less], grad_landed.at[less], sems.at[9]).wait()
    for z in range(outer):
        rows = pl.ds(z * shard, shard)
        total = grad_wide[spot, rows]
        for k in range(1, inner):
            total += grad_landed[lax.rem(spot + k, inner), rows].astype(F32)
        part_wide[z % 2, z // 2] = total
        part_sent[z % 2, z // 2] = total.astype(BF16)
    pair_copy = pltpu.make_async_remote_copy(
        part_sent.at[1 - parity], part_landed, sems.at[10], sems.at[11],
        device_id=(sec, (plane + 1 - 2 * parity) * inner + spot), device_id_type=MESH,
    )
    pair_copy.start()

    collect(1, source_back, back, passed)

    pair_copy.wait_recv()
    pairs = outer // 2
    for h in range(pairs):
        total = part_wide[parity, h] + part_landed[h].astype(F32)
        far_wide[h] = total
        far_sent[h] = total.astype(BF16)

    def send_far(k, carry):
        h = lax.rem(pair + k, pairs)
        pltpu.make_async_remote_copy(
            far_sent.at[h], far_landed.at[pair], sems.at[12], sems.at[13],
            device_id=(sec, (2 * h + parity) * inner + spot), device_id_type=MESH,
        ).start()
        return carry
    lax.fori_loop(1, pairs, send_far, 0)

    few = pl.ds(0, pairs - 1)
    pltpu.make_async_copy(far_sent.at[few], far_landed.at[few], sems.at[13]).wait()
    grad = far_wide[pair]
    for k in range(1, pairs):
        grad += far_landed[lax.rem(pair + k, pairs)].astype(F32)
    for i in (4, 5, 6):
        loads[i].wait()
    first = beta_first * moment[...] + (1.0 - beta_first) * grad
    other = beta_second * second[...] + (1.0 - beta_second) * grad * grad
    update = first / first_correction / (jnp.sqrt(other / second_correction) + adam_eps)
    first_out[...] = first
    second_out[...] = other
    master_out[...] = master[...] - learn_rate * (update + weight_decay * master[...])
    stores = [
        pltpu.make_async_copy(first_out, new_moment, load_sems.at[7]),
        pltpu.make_async_copy(second_out, new_second, load_sems.at[8]),
        pltpu.make_async_copy(master_out, new_master, load_sems.at[9]),
    ]
    for copy in stores:
        copy.start()

    most = pl.ds(0, peers - 1)
    for t, result in ((0, handed), (1, passed)):
        pltpu.make_async_copy(landings[t].at[most], landings[t].at[most], sems.at[t]).wait()
        pltpu.make_async_copy(outgoing.at[t], outgoing.at[t], sems.at[4 + t]).wait()
        pltpu.make_async_copy(result, result, sems.at[6 + t]).wait()
    pltpu.make_async_copy(grad_sent.at[less], grad_sent.at[less], sems.at[8]).wait()
    pair_copy.wait_send()
    pltpu.make_async_copy(far_sent.at[few], far_sent.at[few], sems.at[12]).wait()
    for copy in stores:
        copy.wait()


def deliver(*refs):
    sources, results, staged, arrived, left = refs[:5], refs[5:10], refs[10:15], refs[15], refs[16]
    loads = [pltpu.make_async_copy(sources[i], staged[i], arrived.at[i]) for i in range(5)]
    stores = [pltpu.make_async_copy(staged[i], results[i], left.at[i]) for i in range(5)]
    order = (2, 3, 4, 0, 1)
    for i in order:
        loads[i].start()
    for i in order:
        loads[i].wait()
        stores[i].start()
    for i in order:
        stores[i].wait()


def plane_size(peers):
    size = 1
    while size * size < peers:
        size *= 2
    return size


def shards(sections, arrivals, kept, returned, onward, backward_route, replicas, master, moment, second):
    peers = lax.axis_size("peer")
    token_count, features = arrivals.shape[2:]
    lanes = replicas.shape[3]
    shard = master.shape[1]
    inner = plane_size(peers)
    outer = peers // inner
    col_groups = peers // (token_count // ROWS)
    width = -(-features // (col_groups * 128)) * 128
    padded = width * col_groups
    hbm = pl.BlockSpec(memory_space=pltpu.HBM)
    smem = pl.BlockSpec(memory_space=pltpu.SMEM)
    rows = jax.ShapeDtypeStruct((shard, lanes), F32)
    block = jax.ShapeDtypeStruct((token_count, padded), BF16)
    operands = (
        arrivals[0, 0], kept[0, 0], returned[0, 0], replicas[0, 0], master[0], moment[0], second[0],
    )
    results = pl.pallas_call(
        functools.partial(kernel, sections, peers, inner, width),
        out_shape=(block, block, rows, rows, rows),
        in_specs=[smem] * 2 + [hbm] * 7,
        out_specs=(hbm,) * 5,
        scratch_shapes=[pltpu.VMEM(a.shape, a.dtype) for a in operands] + [
            pltpu.VMEM((2, token_count, padded), BF16),
            pltpu.VMEM((peers, ROWS, width), BF16),
            pltpu.VMEM((peers, ROWS, width), BF16),
            pltpu.VMEM((2, peers, ROWS, width), BF16),
            pltpu.VMEM((token_count, features), F32),
            pltpu.VMEM((2 * token_count, features), BF16),
            pltpu.VMEM((inner, outer * shard, lanes), F32),
            pltpu.VMEM((inner, outer * shard, lanes), BF16),
            pltpu.VMEM((inner, outer * shard, lanes), BF16),
            pltpu.VMEM((2, outer // 2, shard, lanes), F32),
            pltpu.VMEM((2, outer // 2, shard, lanes), BF16),
            pltpu.VMEM((outer // 2, shard, lanes), BF16),
            pltpu.VMEM((outer // 2, shard, lanes), F32),
            pltpu.VMEM((outer // 2, shard, lanes), BF16),
            pltpu.VMEM((outer // 2, shard, lanes), BF16),
            pltpu.VMEM((shard, lanes), F32),
            pltpu.VMEM((shard, lanes), F32),
            pltpu.VMEM((shard, lanes), F32),
            pltpu.SMEM((peers,), jnp.int32),
            pltpu.SMEM((peers,), jnp.int32),
            pltpu.SemaphoreType.DMA((10,)),
            pltpu.SemaphoreType.DMA((14,)),
        ],
        compiler_params=pltpu.CompilerParams(
            collective_id=0, has_side_effects=True, vmem_limit_bytes=64 * 1024 * 1024 - 65536
        ),
        name="routed_step",
    )(
        onward[0], backward_route[0], *operands
    )
    handed, passed, new_master, new_moment, new_second = pl.pallas_call(
        deliver,
        out_shape=(block, block, rows, rows, rows),
        in_specs=[hbm] * 5,
        out_specs=(hbm,) * 5,
        scratch_shapes=[pltpu.VMEM(a.shape, a.dtype) for a in (block, block, rows, rows, rows)]
        + [pltpu.SemaphoreType.DMA((5,)), pltpu.SemaphoreType.DMA((5,))],
        compiler_params=pltpu.CompilerParams(vmem_limit_bytes=64 * 1024 * 1024 - 65536),
        name="deliver",
    )(*results)
    return (
        handed[None, None, :, :features], passed[None, None, :, :features],
        new_master[None], new_moment[None], new_second[None],
    )


def solution(mesh):
    whole = P("section", "peer", None, None)
    rows = P("section", "peer", None)
    table = P("section", None)
    return jax.shard_map(
        functools.partial(shards, mesh.shape["section"]),
        mesh=mesh,
        in_specs=(whole, whole, whole, table, table, whole, rows, rows, rows),
        out_specs=(whole, whole, rows, rows, rows),
        check_vma=False,
    )
```

```python
import functools
import math

import jax
import jax.numpy as jnp
from jax import lax
from jax.experimental import pallas as pl
from jax.experimental.pallas import tpu as pltpu
from jax.sharding import PartitionSpec as P

norm_eps = 1e-05
beta_first = 0.9
beta_second = 0.95
adam_eps = 1e-08
learn_rate = 0.05
weight_decay = 0.1
first_correction = 1.0 - 0.9**10
second_correction = 1.0 - 0.95**10

ROWS = 16
MESH = pl.DeviceIdType.MESH
F32, BF16 = jnp.float32, jnp.bfloat16


def column_chunks(width, parts):
    step = width // parts
    return [(i * step, step) for i in range(parts)]


def kernel(
    sections, peers, inner, width,
    table_on, table_back, *refs,
):
    operands, refs = refs[:7], refs[7:]
    results, refs = refs[:5], refs[5:]
    staged, refs = refs[:7], refs[7:]
    step(sections, peers, inner, width, table_on, table_back, operands, *staged, *results, *refs)


def step(
    sections, peers, inner, width, table_on, table_back, operands,
    arrivals, kept, returned, weights, master, moment, second,
    handed, passed, new_master, new_moment, new_second,
    made, landed_on, landed_back, outgoing, grad_normed, stacked, grad_wide, grad_sent, grad_landed,
    part_wide, part_sent, part_landed, far_wide, far_sent, far_landed,
    first_out, second_out, master_out, source_on, source_back, load_sems, sems,
):
    token_count, features = arrivals.shape
    rank = weights.shape[1] // 2
    outer = peers // inner
    col_groups = peers // (token_count // ROWS)
    shard = master.shape[0]
    sec, me = lax.axis_index("section"), lax.axis_index("peer")
    plane, spot = me // inner, lax.rem(me, inner)
    onto = lax.rem(sec + 1, sections)
    back = lax.rem(sec + sections - 1, sections)

    loads = [
        pltpu.make_async_copy(operand, here, load_sems.at[i])
        for i, (operand, here) in enumerate(
            zip(operands, (arrivals, kept, returned, weights, master, moment, second))
        )
    ]
    for i in (0, 3, 1, 2, 4, 5, 6):
        loads[i].start()
    landings = (landed_on, landed_back)
    barrier = pltpu.get_barrier_semaphore()

    def greet(section, first):
        def one(k, carry):
            target = lax.rem(me + k, peers)
            pl.semaphore_signal(barrier, inc=1, device_id=(section, target), device_id_type=MESH)
            return carry
        lax.fori_loop(first, peers, one, 0)

    greet(sec, 1)
    greet(onto, 0)
    greeted = 2 * peers - 1
    if sections > 2:
        greet(back, 0)
        greeted += peers

    def piece(j):
        row = pl.multiple_of((j // col_groups) * ROWS, ROWS)
        col = pl.multiple_of(lax.rem(j, col_groups) * width, 128)
        return pl.ds(row, ROWS), pl.ds(col, width)

    def spread(t):
        def one(k, carry):
            j = lax.rem(me + k, peers)
            rows, cols = piece(j)
            pltpu.make_async_remote_copy(
                made.at[t, rows, cols], landings[t].at[me], sems.at[t], sems.at[2 + t],
                device_id=(sec, j), device_id_type=MESH,
            ).start()
            return carry
        lax.fori_loop(1, peers, one, 0)
        rows, cols = piece(me)
        pltpu.make_async_copy(made.at[t, rows, cols], landings[t].at[me], sems.at[2 + t]).start()

    def collect(t, order, section, result):
        pltpu.make_async_copy(landings[t], landings[t], sems.at[2 + t]).wait()
        rows, cols = piece(me)

        def one(k, carry):
            d = lax.rem(me + k, peers)
            outgoing[t, d] = landings[t][order[d]]
            pltpu.make_async_remote_copy(
                outgoing.at[t, d], result.at[rows, cols], sems.at[4 + t], sems.at[6 + t],
                device_id=(section, d), device_id_type=MESH,
            ).start()
            return carry
        lax.fori_loop(0, peers, one, 0)

    def invert(table, order):
        def one(d, carry):
            found = jnp.int32(0)
            for p in range(1, peers):
                found = jnp.where(table[p] == d, p, found)
            order[d] = found
            return carry
        lax.fori_loop(0, peers, one, 0)

    chunks = column_chunks(features, 4)
    if made.shape[2] > features:
        made[:, :, features:] = jnp.zeros((2, token_count, made.shape[2] - features), BF16)

    def rate(ref):
        total = jnp.zeros((token_count, 128), F32)
        for start, size in chunks:
            x = ref[:, start:start + size].astype(F32)
            x = x * x
            for c in range(0, size, 128):
                total += x[:, c:c + 128]
        return lax.rsqrt(jnp.sum(total, axis=1, keepdims=True) * (1.0 / features) + norm_eps)

    right = lax.broadcasted_iota(jnp.int32, (token_count, 2 * rank), 1) >= rank
    nt = (((1,), (1,)), ((), ()))

    loads[0].wait()
    r = rate(arrivals)
    loads[3].wait()
    hidden = jnp.zeros((token_count, 2 * rank), F32)
    for start, size in chunks:
        normed = (arrivals[:, start:start + size].astype(F32) * r).astype(BF16)
        hidden += jnp.dot(normed, weights[start:start + size, :], preferred_element_type=F32)
    hidden = hidden * features ** (-0.5)
    active = hidden / (1.0 + jnp.exp(-hidden))
    active = jnp.where(right, pltpu.roll(active, rank, 1), 0.0).astype(BF16)
    pieced = width * col_groups == features and col_groups <= 4
    if not pieced:
        for start, size in chunks:
            branch = lax.dot_general(active, weights[start:start + size, :], nt, preferred_element_type=F32)
            y = arrivals[:, start:start + size].astype(F32) + branch * rank ** (-0.5)
            made[0, :, start:start + size] = y.astype(BF16)
        pl.semaphore_wait(barrier, greeted)
        spread(0)
    else:
        row_groups = peers // col_groups
        for i in range(col_groups):
            group = lax.rem(me + i, col_groups)
            part = pl.ds(pl.multiple_of(group * width, 128), width)
            branch = lax.dot_general(active, weights[part, :], nt, preferred_element_type=F32)
            y = arrivals[:, part].astype(F32) + branch * rank ** (-0.5)
            made[0, :, part] = y.astype(BF16)
            if i == 0:
                pl.semaphore_wait(barrier, greeted)

            def one(k, carry):
                j = lax.rem(me // col_groups + k, row_groups) * col_groups + group
                rows, cols = piece(j)
                pltpu.make_async_remote_copy(
                    made.at[0, rows, cols], landed_on.at[me], sems.at[0], sems.at[2],
                    device_id=(sec, j), device_id_type=MESH,
                ).start()
                return carry
            lax.fori_loop(1 if i == 0 else 0, row_groups, one, 0)
        rows, cols = piece(me)
        pltpu.make_async_copy(made.at[0, rows, cols], landed_on.at[me], sems.at[2]).start()

    loads[1].wait()
    loads[2].wait()
    r = rate(kept)
    both = jnp.zeros((2 * token_count, 2 * rank), F32)
    for start, size in chunks:
        normed = (kept[:, start:start + size].astype(F32) * r).astype(BF16)
        stacked[:token_count, start:start + size] = normed
        stacked[token_count:, start:start + size] = returned[:, start:start + size]
        both += jnp.dot(stacked[:, start:start + size], weights[start:start + size, :], preferred_element_type=F32)
    hidden = both[:token_count] * features ** (-0.5)
    grad_active = pltpu.roll(both[token_count:], rank, 1) * rank ** (-0.5)
    logistic = 1.0 / (1.0 + jnp.exp(-hidden))
    active = jnp.where(right, pltpu.roll(hidden * logistic, rank, 1), 0.0).astype(BF16)
    grad_hidden = grad_active * logistic * (1.0 + hidden * (1.0 - logistic))
    grad_hidden = jnp.where(right, 0.0, grad_hidden).astype(BF16)
    mixed = jnp.zeros((token_count, 128), F32)
    for start, size in chunks:
        g = lax.dot_general(grad_hidden, weights[start:start + size, :], nt, preferred_element_type=F32)
        g = g * features ** (-0.5)
        grad_normed[:, start:start + size] = g
        g = g * kept[:, start:start + size].astype(F32)
        for c in range(0, size, 128):
            mixed += g[:, c:c + 128]
    mixed = jnp.sum(mixed, axis=1, keepdims=True) * (1.0 / features)
    pull = r * r * r * mixed
    for start, size in chunks:
        dx = (
            returned[:, start:start + size].astype(F32)
            + r * grad_normed[:, start:start + size]
            - kept[:, start:start + size].astype(F32) * pull
        )
        made[1, :, start:start + size] = dx.astype(BF16)
    spread(1)

    factors = jnp.concatenate([grad_hidden, active], axis=0)
    scale = jnp.where(
        lax.broadcasted_iota(jnp.int32, (1, 2 * rank), 1) >= rank, rank ** (-0.5), features ** (-0.5)
    )
    step = math.lcm(shard, 128)
    for start in range(0, features, step):
        g = lax.dot_general(
            stacked[:, start:start + step], factors, (((0,), (0,)), ((), ())), preferred_element_type=F32
        ) * scale
        for i in range(step // shard):
            j = start // shard + i
            z, q = divmod(j, inner)
            rows = g[i * shard:(i + 1) * shard]
            grad_wide[q, z * shard:(z + 1) * shard] = rows
            grad_sent[q, z * shard:(z + 1) * shard] = rows.astype(BF16)

    def send_plane(k, carry):
        q = lax.rem(spot + k, inner)
        pltpu.make_async_remote_copy(
            grad_sent.at[q], grad_landed.at[spot], sems.at[8], sems.at[9],
            device_id=(sec, plane * inner + q), device_id_type=MESH,
        ).start()
        return carry
    lax.fori_loop(1, inner, send_plane, 0)

    invert(table_on, source_on)
    invert(table_back, source_back)
    collect(0, source_on, onto, handed)

    parity, pair = lax.rem(plane, 2), plane // 2
    less = pl.ds(0, inner - 1)
    pltpu.make_async_copy(grad_sent.at[less], grad_landed.at[less], sems.at[9]).wait()
    for z in range(outer):
        rows = pl.ds(z * shard, shard)
        total = grad_wide[spot, rows]
        for k in range(1, inner):
            total += grad_landed[lax.rem(spot + k, inner), rows].astype(F32)
        part_wide[z % 2, z // 2] = total
        part_sent[z % 2, z // 2] = total.astype(BF16)
    pair_copy = pltpu.make_async_remote_copy(
        part_sent.at[1 - parity], part_landed, sems.at[10], sems.at[11],
        device_id=(sec, (plane + 1 - 2 * parity) * inner + spot), device_id_type=MESH,
    )
    pair_copy.start()

    pair_copy.wait_recv()
    pairs = outer // 2
    for h in range(pairs):
        total = part_wide[parity, h] + part_landed[h].astype(F32)
        far_wide[h] = total
        far_sent[h] = total.astype(BF16)

    def send_far(k, carry):
        h = lax.rem(pair + k, pairs)
        pltpu.make_async_remote_copy(
            far_sent.at[h], far_landed.at[pair], sems.at[12], sems.at[13],
            device_id=(sec, (2 * h + parity) * inner + spot), device_id_type=MESH,
        ).start()
        return carry
    lax.fori_loop(1, pairs, send_far, 0)

    collect(1, source_back, back, passed)

    few = pl.ds(0, pairs - 1)
    pltpu.make_async_copy(far_sent.at[few], far_landed.at[few], sems.at[13]).wait()
    grad = far_wide[pair]
    for k in range(1, pairs):
        grad += far_landed[lax.rem(pair + k, pairs)].astype(F32)
    for i in (4, 5, 6):
        loads[i].wait()
    first = beta_first * moment[...] + (1.0 - beta_first) * grad
    other = beta_second * second[...] + (1.0 - beta_second) * grad * grad
    update = first / first_correction / (jnp.sqrt(other / second_correction) + adam_eps)
    first_out[...] = first
    second_out[...] = other
    master_out[...] = master[...] - learn_rate * (update + weight_decay * master[...])
    stores = [
        pltpu.make_async_copy(first_out, new_moment, load_sems.at[7]),
        pltpu.make_async_copy(second_out, new_second, load_sems.at[8]),
        pltpu.make_async_copy(master_out, new_master, load_sems.at[9]),
    ]
    for copy in stores:
        copy.start()

    most = pl.ds(0, peers - 1)
    for t, result in ((0, handed), (1, passed)):
        pltpu.make_async_copy(landings[t].at[most], landings[t].at[most], sems.at[t]).wait()
        pltpu.make_async_copy(outgoing.at[t], outgoing.at[t], sems.at[4 + t]).wait()
        pltpu.make_async_copy(result, result, sems.at[6 + t]).wait()
    pltpu.make_async_copy(grad_sent.at[less], grad_sent.at[less], sems.at[8]).wait()
    pair_copy.wait_send()
    pltpu.make_async_copy(far_sent.at[few], far_sent.at[few], sems.at[12]).wait()
    for copy in stores:
        copy.wait()


def deliver(*refs):
    sources, results, staged, arrived, left = refs[:5], refs[5:10], refs[10:15], refs[15], refs[16]
    loads = [pltpu.make_async_copy(sources[i], staged[i], arrived.at[i]) for i in range(5)]
    stores = [pltpu.make_async_copy(staged[i], results[i], left.at[i]) for i in range(5)]
    order = (2, 3, 4, 0, 1)
    for i in order:
        loads[i].start()
    for i in order:
        loads[i].wait()
        stores[i].start()
    for i in order:
        stores[i].wait()


def plane_size(peers):
    size = 1
    while size * size < peers:
        size *= 2
    return size


def shards(sections, arrivals, kept, returned, onward, backward_route, replicas, master, moment, second):
    peers = lax.axis_size("peer")
    token_count, features = arrivals.shape[2:]
    lanes = replicas.shape[3]
    shard = master.shape[1]
    inner = plane_size(peers)
    outer = peers // inner
    col_groups = peers // (token_count // ROWS)
    width = -(-features // (col_groups * 128)) * 128
    padded = width * col_groups
    hbm = pl.BlockSpec(memory_space=pltpu.HBM)
    smem = pl.BlockSpec(memory_space=pltpu.SMEM)
    rows = jax.ShapeDtypeStruct((shard, lanes), F32)
    block = jax.ShapeDtypeStruct((token_count, padded), BF16)
    operands = (
        arrivals[0, 0], kept[0, 0], returned[0, 0], replicas[0, 0], master[0], moment[0], second[0],
    )
    results = pl.pallas_call(
        functools.partial(kernel, sections, peers, inner, width),
        out_shape=(block, block, rows, rows, rows),
        in_specs=[smem] * 2 + [hbm] * 7,
        out_specs=(hbm,) * 5,
        scratch_shapes=[pltpu.VMEM(a.shape, a.dtype) for a in operands] + [
            pltpu.VMEM((2, token_count, padded), BF16),
            pltpu.VMEM((peers, ROWS, width), BF16),
            pltpu.VMEM((peers, ROWS, width), BF16),
            pltpu.VMEM((2, peers, ROWS, width), BF16),
            pltpu.VMEM((token_count, features), F32),
            pltpu.VMEM((2 * token_count, features), BF16),
            pltpu.VMEM((inner, outer * shard, lanes), F32),
            pltpu.VMEM((inner, outer * shard, lanes), BF16),
            pltpu.VMEM((inner, outer * shard, lanes), BF16),
            pltpu.VMEM((2, outer // 2, shard, lanes), F32),
            pltpu.VMEM((2, outer // 2, shard, lanes), BF16),
            pltpu.VMEM((outer // 2, shard, lanes), BF16),
            pltpu.VMEM((outer // 2, shard, lanes), F32),
            pltpu.VMEM((outer // 2, shard, lanes), BF16),
            pltpu.VMEM((outer // 2, shard, lanes), BF16),
            pltpu.VMEM((shard, lanes), F32),
            pltpu.VMEM((shard, lanes), F32),
            pltpu.VMEM((shard, lanes), F32),
            pltpu.SMEM((peers,), jnp.int32),
            pltpu.SMEM((peers,), jnp.int32),
            pltpu.SemaphoreType.DMA((10,)),
            pltpu.SemaphoreType.DMA((14,)),
        ],
        compiler_params=pltpu.CompilerParams(
            collective_id=0, has_side_effects=True, vmem_limit_bytes=64 * 1024 * 1024 - 65536
        ),
        name="routed_step",
    )(
        onward[0], backward_route[0], *operands
    )
    handed, passed, new_master, new_moment, new_second = pl.pallas_call(
        deliver,
        out_shape=(block, block, rows, rows, rows),
        in_specs=[hbm] * 5,
        out_specs=(hbm,) * 5,
        scratch_shapes=[pltpu.VMEM(a.shape, a.dtype) for a in (block, block, rows, rows, rows)]
        + [pltpu.SemaphoreType.DMA((5,)), pltpu.SemaphoreType.DMA((5,))],
        compiler_params=pltpu.CompilerParams(vmem_limit_bytes=64 * 1024 * 1024 - 65536),
        name="deliver",
    )(*results)
    return (
        handed[None, None, :, :features], passed[None, None, :, :features],
        new_master[None], new_moment[None], new_second[None],
    )


def solution(mesh):
    whole = P("section", "peer", None, None)
    rows = P("section", "peer", None)
    table = P("section", None)
    return jax.shard_map(
        functools.partial(shards, mesh.shape["section"]),
        mesh=mesh,
        in_specs=(whole, whole, whole, table, table, whole, rows, rows, rows),
        out_specs=(whole, whole, rows, rows, rows),
        check_vma=False,
    )
```
